128 devices in a mesh: span: 8 (over x_hi, z), seq: 16 (over x_lo, y, core).
Axes of the slice: x: 4 (x_hi: 2, x_lo: 2; x = x_hi * 2 + x_lo), y: 4, z: 4, core: 2. Of those that a mesh axis runs over, the one named last changes fastest.
Arguments:
- projected: bfloat16 [8, 2048, 8192], P('span', 'seq'), may hold values from -7 to 7
- cache_kv: bfloat16 [2048, 2, 1024], P('seq'), may hold values from -6 to 6
- levels: int32 [8], P('span'), may hold values from 0 to 15
- cache_blocks: int32 [8], P('span'), may hold values from 1 to 16, as said below
- gate_table: float32 [16, 6144], P(None, 'seq'), may hold values from 0.1 to 1.9
Outputs:
- gated: bfloat16 [8, 2048, 6144], P('span', 'seq')
The draws below stay inside these ranges and needn't reach their ends.
Inputs may be any that keep to these rules, and one draw needn't show every extreme that they name: `cache_blocks`: nondecreasing along the spans; the last span's entry equals 16.
All inputs are finite; a program needn't handle non-finite values.
Results may differ from the reference program's by a relative error of at most 0.0095.
Values may be sent and summed in bfloat16 or wider, within the bound.
A program may use at most 128 MiB of HBM per device.

```python
import jax
import jax.numpy as jnp
from jax import lax

MODEL_WIDTH = 6144
HEAD_DIM = 128
KV_GROUPS = 8
CACHED = 2048
WINDOW = 2
CACHE_BLOCK = 128
LEVELS = 16
KV_WIDTH = 1024
SPAN_TOKENS = 2048
SPANS = 8


def draw_projected(key, part):
    key = jax.random.fold_in(key, 3)
    base_key = jax.random.fold_in(key, 0)
    kv_width = KV_GROUPS * HEAD_DIM
    shape = (SPANS, SPAN_TOKENS, MODEL_WIDTH + 2 * kv_width)
    return jnp.clip(jax.random.normal(base_key, shape, jnp.float32), -4.0, 4.0).astype(jnp.bfloat16)


def draw_cache_blocks(key, part):
    key = jax.random.fold_in(key, 7)
    most_blocks = CACHED // CACHE_BLOCK
    drawn = jax.random.randint(key, (SPANS,), 1, most_blocks + 1)
    ordered = jnp.sort(drawn)
    return ordered.at[SPANS - 1].set(most_blocks).astype(jnp.int32)


def touch_ends(values, key, smallest, top_value):
    shape = values.shape
    spot = [jax.random.randint(jax.random.fold_in(key, axis), (), 0, shape[axis]) for axis in range(len(shape))]
    values = values.at[tuple(spot)].set(smallest)
    longest = shape.index(max(shape))
    spot[longest] = (spot[longest] + 1) % shape[longest]
    return values.at[tuple(spot)].set(top_value)


def block_scale(key, extent, cuts, smallest, high):
    def one(dim, parts):
        heights = jax.random.uniform(jax.random.fold_in(jax.random.fold_in(key, 6), dim), (parts,), jnp.float32, smallest / len(cuts), high / len(cuts))
        return jnp.repeat(jnp.exp(heights), extent[dim] // parts).reshape((-1,) + (1,) * (len(extent) - dim - 1))

    factor_of = one(*cuts[0])
    for cut in cuts[1:]:
        factor_of = factor_of * one(*cut)
    return factor_of


def gaussian(stream_key, dims, deviation, reach, cuts=(), kind=jnp.bfloat16):
    gain = block_scale(stream_key, dims, cuts, -0.22, 0.18) if cuts else 1.0
    values = jax.random.normal(stream_key, dims, jnp.float32) * deviation * gain
    return jnp.minimum(jnp.maximum(values, -reach), reach).astype(kind)


def setup_inputs(seed: int = 0) -> dict:
    arg_keys = jax.random.split(jax.random.key(seed), 6)
    projected = draw_projected(jax.random.fold_in(arg_keys[5], 71), 0)
    cache_kv = gaussian(arg_keys[1], (CACHED, 2, KV_WIDTH), 1.0, 6.0, ((0, 16),))
    levels = touch_ends(jax.random.randint(arg_keys[2], (SPANS,), 0, LEVELS), jax.random.fold_in(arg_keys[2], 1), 0, LEVELS - 1).astype(jnp.int32)
    cache_blocks = draw_cache_blocks(jax.random.fold_in(arg_keys[5], 71), 0)
    gate_table = jnp.clip(1.0 + 0.18 * jax.random.normal(arg_keys[4], (LEVELS, MODEL_WIDTH), jnp.float32), 0.1, 1.9)
    return {"projected": projected, "cache_kv": cache_kv, "levels": levels, "cache_blocks": cache_blocks, "gate_table": gate_table}


NEGATIVE = -1e+30

def attend_head(queries, key_rows, value_rows, allowed, score_scale):
    scores = jnp.dot(queries, jnp.transpose(key_rows), preferred_element_type=jnp.float32) * score_scale
    scores = jnp.where(allowed[None, :], scores, NEGATIVE)
    row_best = lax.optimization_barrier(jnp.max(scores, axis=-1, keepdims=True))
    weights = jnp.exp(scores - row_best)
    row_total = lax.optimization_barrier(jnp.sum(weights, axis=-1, keepdims=True))
    summed = jnp.dot(weights.astype(jnp.bfloat16), value_rows, preferred_element_type=jnp.float32)
    return summed / row_total

def reference(projected, cache_kv, levels, cache_blocks, gate_table):
    score_scale = HEAD_DIM ** (-0.5)
    head_total = MODEL_WIDTH // HEAD_DIM
    per_group = head_total // KV_GROUPS
    kv_width = KV_GROUPS * HEAD_DIM
    cache_keys = cache_kv[:, 0].reshape(CACHED, KV_GROUPS, HEAD_DIM)
    cache_values = cache_kv[:, 1].reshape(CACHED, KV_GROUPS, HEAD_DIM)
    positions = jnp.arange(CACHED, dtype=jnp.int32)
    outputs = []
    for group in range(SPANS):
        rows_here = projected[group]
        key_parts = [rows_here[:, MODEL_WIDTH:MODEL_WIDTH + kv_width].reshape(SPAN_TOKENS, KV_GROUPS, HEAD_DIM)]
        value_parts = [rows_here[:, MODEL_WIDTH + kv_width:].reshape(SPAN_TOKENS, KV_GROUPS, HEAD_DIM)]
        flag_parts = [jnp.ones((SPAN_TOKENS,), dtype=jnp.bool_)]
        for distance in range(1, WINDOW + 1):
            if group - distance >= 0:
                earlier = projected[group - distance]
                key_parts.append(earlier[:, MODEL_WIDTH:MODEL_WIDTH + kv_width].reshape(SPAN_TOKENS, KV_GROUPS, HEAD_DIM))
                value_parts.append(earlier[:, MODEL_WIDTH + kv_width:].reshape(SPAN_TOKENS, KV_GROUPS, HEAD_DIM))
                flag_parts.append(jnp.ones((SPAN_TOKENS,), dtype=jnp.bool_))
        key_parts.append(cache_keys)
        value_parts.append(cache_values)
        flag_parts.append(positions < cache_blocks[group] * CACHE_BLOCK)
        all_keys = jnp.transpose(jnp.repeat(jnp.concatenate(key_parts, axis=0), per_group, axis=1), (1, 0, 2))
        all_values = jnp.transpose(jnp.repeat(jnp.concatenate(value_parts, axis=0), per_group, axis=1), (1, 0, 2))
        allowed = jnp.concatenate(flag_parts, axis=0)
        queries = jnp.transpose(rows_here[:, :MODEL_WIDTH].reshape(SPAN_TOKENS, head_total, HEAD_DIM), (1, 0, 2))

        def per_head(head_item):
            return attend_head(head_item[0], head_item[1], head_item[2], allowed, score_scale)
        attended = lax.map(per_head, (queries, all_keys, all_values))
        normed = attended * lax.rsqrt(lax.optimization_barrier(jnp.mean(attended * attended, axis=-1, keepdims=True)) + 1e-06)
        flat = jnp.transpose(normed, (1, 0, 2)).reshape(SPAN_TOKENS, MODEL_WIDTH)
        gate_row = gate_table[levels[group]]
        outputs.append((flat * gate_row[None, :]).astype(jnp.bfloat16))
    return jnp.stack(outputs)
```

```python
import functools

import jax
import jax.numpy as jnp
from jax import lax
from jax.experimental import pallas as pl
from jax.experimental.pallas import tpu as pltpu
from jax.sharding import PartitionSpec as P

MODEL_WIDTH = 6144
HEAD_DIM = 128
KV_WIDTH = 1024
SPANS = 8
SEQ = 16
TOK = 128
HEADS = 3
QW = HEADS * HEAD_DIM
SPAN_TOKENS = 2048
HALF = SPAN_TOKENS // 2
CHUNK = 512
BQ = 512
QBLOCKS = 12
SUB = 512
NEGATIVE = -1e30
MASKED = 1e30
SCALE = HEAD_DIM ** -0.5 * 1.4426950408889634
OWN, CACHE, NEAR, FAR = range(4)
MESH = pl.DeviceIdType.MESH

CACHE_STEP = 7
NEAR_STEPS = (6, 11)
FAR_STEPS = (17, 22)


def kernel(
    x, cache, levels, blocks, gate, out,
    kv, vt, qin, qt, acc, top, total, s0, s1, stage, gates,
    kv_send, kv_recv, local_sem, side_send, side_recv, pass_send, pass_recv,
    q_send, q_recv, out_send, out_recv, out_local,
):
    c = lax.axis_index("span")
    s = lax.axis_index("seq")
    chip = s // 2
    core = s % 2
    xlo = chip // 4
    y = chip % 4
    group = s // 4
    limit = blocks[0]
    windows = jnp.minimum(c, 2)
    ways = jnp.maximum(windows, 1)
    steps = 2 * QBLOCKS + QBLOCKS * windows
    beside = {"span": c, "seq": 2 * chip + (1 - core)}
    after = {"span": jnp.minimum(c + 1, SPANS - 1), "seq": s}

    barrier = pltpu.get_barrier_semaphore()
    for d in range(1, SEQ):
        pl.semaphore_signal(barrier, inc=1, device_id={"span": c, "seq": (s + d) % SEQ}, device_id_type=MESH)

    @pl.when(c > 0)
    def _():
        pl.semaphore_signal(barrier, inc=1, device_id={"span": jnp.maximum(c - 1, 0), "seq": s}, device_id_type=MESH)

    @pl.when(c < SPANS - 1)
    def _():
        pl.semaphore_signal(barrier, inc=1, device_id=after, device_id_type=MESH)

    pl.semaphore_wait(barrier, SEQ - 1 + jnp.where(c > 0, 1, 0) + jnp.where(c < SPANS - 1, 1, 0))

    def source(stream, which, head):
        if stream == OWN:
            return x.at[0, :, pl.ds(pl.multiple_of(MODEL_WIDTH + KV_WIDTH * which + HEAD_DIM * head, 128), HEAD_DIM)]
        return cache.at[:, pl.ds(pl.multiple_of(KV_WIDTH * which + HEAD_DIM * head, 128), HEAD_DIM)]

    def send_kv(stream):
        piece = pl.ds(pl.multiple_of(TOK * chip, TOK), TOK)
        for dx, dy in ((0, 1), (0, 3), (0, 2), (1, 0), (1, 1), (1, 3), (1, 2)):
            there = ((xlo + dx) % 2) * 4 + (y + dy) % 4
            for which in range(2):
                pltpu.make_async_remote_copy(
                    src_ref=source(stream, which, there),
                    dst_ref=kv.at[stream, core, which, piece],
                    send_sem=kv_send.at[stream],
                    recv_sem=kv_recv.at[stream, xlo],
                    device_id={"span": c, "seq": 2 * there + core},
                    device_id_type=MESH,
                ).start()
        for which in range(2):
            pltpu.make_async_copy(source(stream, which, chip), kv.at[stream, core, which, piece], local_sem.at[stream]).start()

    def group_at(turn):
        return ((group // 2 + turn // 2) % 2) * 2 + (group % 2 + turn % 2) % 2

    def send_q(turn):
        for e in range(4):
            there = 4 * group_at(turn) + (s % 4 + e) % 4
            wanted = x.at[0, :, pl.ds(pl.multiple_of(QW * there, 128), QW)]
            if turn == 0 and e == 0:
                pltpu.make_async_copy(wanted, qin.at[s], local_sem.at[2]).start()
            else:
                pltpu.make_async_remote_copy(
                    src_ref=wanted,
                    dst_ref=qin.at[s],
                    send_sem=q_send,
                    recv_sem=q_recv.at[group],
                    device_id={"span": c, "seq": there},
                    device_id_type=MESH,
                ).start()

    send_kv(OWN)
    send_q(0)
    send_q(1)
    send_q(2)
    send_kv(CACHE)
    send_q(3)

    def clear(i, unused):
        acc[i] = jnp.zeros((HEAD_DIM, BQ), jnp.float32)
        total[i] = jnp.zeros((8, BQ), jnp.float32)
        top[i] = jnp.full((8, BQ), NEGATIVE, jnp.float32)
        return unused

    lax.fori_loop(0, QBLOCKS, clear, 0)
    level_rows = lax.broadcasted_iota(jnp.int32, gate.shape, 0)
    chosen = jnp.sum(jnp.where(level_rows == levels[0], gate[...], 0.0), axis=0, keepdims=True)
    gates[...] = jnp.broadcast_to(chosen, gates.shape)

    def wait_bytes(ref, sem):
        pltpu.make_async_copy(ref, ref, sem).wait()

    def half_rows(part):
        return pl.ds(pl.multiple_of(CHUNK * part, CHUNK), CHUNK)

    def side_copy(stream, part):
        piece = kv.at[stream, core, :, half_rows(part)]
        return pltpu.make_async_remote_copy(
            src_ref=piece, dst_ref=piece, send_sem=side_send.at[stream, part], recv_sem=side_recv.at[stream, part],
            device_id=beside, device_id_type=MESH,
        )

    def pass_copy(stream, part):
        return pltpu.make_async_remote_copy(
            src_ref=kv.at[stream, core, :, half_rows(part)],
            dst_ref=kv.at[FAR if stream == NEAR else NEAR, core, :, half_rows(part)],
            send_sem=pass_send.at[stream // 2, part], recv_sem=pass_recv.at[stream // 2, part],
            device_id=after, device_id_type=MESH,
        )

    def take_kv(stream, first):
        part = xlo if first else 1 - xlo
        if first:
            wait_bytes(kv.at[stream, core, :, pl.ds(0, TOK)], local_sem.at[stream])
        rows = 3 * TOK if first else 4 * TOK
        wait_bytes(kv.at[stream, core, :, pl.ds(0, rows)], kv_recv.at[stream, part])
        side_copy(stream, part).start()
        if stream == OWN:
            @pl.when(c < SPANS - 1)
            def _():
                pass_copy(OWN, part).start()

    def take_window(stream, first):
        part = xlo if first else 1 - xlo
        wait_bytes(kv.at[stream, core, :, pl.ds(0, CHUNK)], pass_recv.at[0 if stream == NEAR else 1, part])
        side_copy(stream, part).start()
        if stream == NEAR:
            @pl.when(c < SPANS - 1)
            def _():
                pass_copy(NEAR, part).start()

    def take_side(stream):
        for part in range(2):
            wait_bytes(kv.at[stream, 1 - core, :, pl.ds(0, CHUNK)], side_recv.at[stream, part])
        for p in range(2):
            for b in range(0, HALF, 512):
                values = kv[stream, p, 1, pl.ds(b, 512), :]
                vt[stream, :, pl.ds(p * HALF + b, 512)] = jnp.transpose(values)

    def take_q(i):
        g = group_at(i // HEADS)

        @pl.when(i == 0)
        def _():
            wait_bytes(qin.at[0], local_sem.at[2])
            wait_bytes(qin.at[pl.ds(0, 3)], q_recv.at[g])

        @pl.when((i > 0) & (i % HEADS == 0))
        def _():
            wait_bytes(qin.at[pl.ds(0, 4)], q_recv.at[g])

        h = i % HEADS
        rows = qin[pl.ds(4 * g, 4), :, pl.ds(pl.multiple_of(h * HEAD_DIM, 128), HEAD_DIM)].reshape(BQ, HEAD_DIM)
        scaled = jnp.transpose(rows.astype(jnp.float32) * SCALE)
        high = scaled.astype(jnp.bfloat16)
        qt[i, pl.ds(0, 128), :] = high
        qt[i, pl.ds(128, 128), :] = (scaled - high.astype(jnp.float32)).astype(jnp.bfloat16)

    def place(t):
        late = t - 2 * QBLOCKS
        early = t < 2 * QBLOCKS
        stream = jnp.where(early, t // QBLOCKS, NEAR + late % ways)
        block = jnp.where(early, t % QBLOCKS, late // ways)
        return stream, block

    def masked(stream, p, piece):
        return jnp.where((stream == CACHE) & (2 * piece + p >= limit), MASKED, 0.0).astype(jnp.float32)

    def scores(t, into):
        stream, block = place(t)
        queries = qt[block]
        best = None
        for ch in range(SPAN_TOKENS // SUB):
            p, start = divmod(ch * SUB, HALF)
            keys = kv[stream, p, 0, pl.ds(start, SUB), :]
            part = jnp.dot(jnp.concatenate([keys, keys], axis=1), queries, preferred_element_type=jnp.float32)
            into[pl.ds(ch * SUB, SUB), :] = part
            for b in range(SUB // TOK):
                here = jnp.max(part[b * TOK:(b + 1) * TOK].reshape(TOK // 8, 8, BQ), axis=0)
                here = here - masked(stream, p, (start + b * TOK) // TOK)
                best = here if best is None else jnp.maximum(best, here)
        best = jnp.max(best, axis=0, keepdims=True)
        old = top[block, 0:1, :]
        return old, jnp.maximum(old, best)

    def arrivals(t):
        @pl.when(t < QBLOCKS)
        def _():
            take_q(t)

        @pl.when(t == CACHE_STEP)
        def _():
            take_kv(CACHE, True)
            take_kv(CACHE, False)

        for which, at in enumerate(NEAR_STEPS):
            @pl.when((t == at) & (c >= 1))
            def _(which=which):
                take_window(NEAR, which == 0)

        for which, at in enumerate(FAR_STEPS):
            @pl.when((t == at) & (c >= 2))
            def _(which=which):
                take_window(FAR, which == 0)

        @pl.when(t == QBLOCKS)
        def _():
            take_side(CACHE)

        @pl.when((t == 2 * QBLOCKS) & (c >= 1))
        def _():
            take_side(NEAR)

        @pl.when((t == 2 * QBLOCKS + 1) & (c >= 2))
        def _():
            take_side(FAR)

    def finish(block):
        summed = acc[block]
        whole = jnp.sum(total[block], axis=0, keepdims=True)
        square = jnp.mean(summed * summed, axis=0, keepdims=True)
        normed = summed * lax.rsqrt(square + 1e-06 * (whole * whole))
        h = block % HEADS
        g = group_at(block // HEADS)
        row = gates[0:1, pl.ds(pl.multiple_of(h * HEAD_DIM, 128), HEAD_DIM)]
        stage[block] = (jnp.transpose(normed) * row).astype(jnp.bfloat16)
        wanted = out.at[0, :, pl.ds(pl.multiple_of((HEADS * s + h) * HEAD_DIM, 128), HEAD_DIM)]
        for e in range(4):
            there = 4 * g + e
            held = stage.at[block, pl.ds(e * TOK, TOK)]

            @pl.when(there == s)
            def _():
                pltpu.make_async_copy(held, wanted, out_local).start()

            @pl.when(there != s)
            def _():
                pltpu.make_async_remote_copy(
                    src_ref=held, dst_ref=wanted, send_sem=out_send, recv_sem=out_recv,
                    device_id={"span": c, "seq": there}, device_id_type=MESH,
                ).start()

    def step(t, now, later, best):
        old, new = best
        stream, block = place(t)
        top[block, 0:1, :] = new
        following = jnp.minimum(t + 1, steps - 1)

        @pl.when(t + 1 < steps)
        def _():
            arrivals(t + 1)

        best = scores(following, later)
        factor = jnp.exp2(old - new)
        update = None
        sums = None
        for ch in range(SPAN_TOKENS // SUB):
            p, start = divmod(ch * SUB, HALF)
            rounded = []
            for b in range(SUB // TOK):
                shift = new + masked(stream, p, (start + b * TOK) // TOK)
                weights = jnp.exp2(now[pl.ds(ch * SUB + b * TOK, TOK), :] - shift)
                part = jnp.sum(weights.reshape(TOK // 8, 8, BQ), axis=0)
                sums = part if sums is None else sums + part
                rounded.append(weights.astype(jnp.bfloat16))
            product = jnp.dot(
                vt[stream, :, pl.ds(ch * SUB, SUB)], jnp.concatenate(rounded, axis=0), preferred_element_type=jnp.float32
            )
            update = product if update is None else update + product
        acc[block] = acc[block] * factor + update
        total[block] = total[block] * factor + sums
        last_one = jnp.where(windows == 0, (t >= QBLOCKS) & (t < 2 * QBLOCKS), (t >= 2 * QBLOCKS) & (stream == NEAR + ways - 1))

        @pl.when(last_one)
        def _():
            finish(block)

        return best

    take_kv(OWN, True)
    take_kv(OWN, False)
    take_q(jnp.int32(0))
    take_side(OWN)
    best = scores(jnp.int32(0), s0)

    def pair(i, best):
        best = step(2 * i, s0, s1, best)
        return step(2 * i + 1, s1, s0, best)

    lax.fori_loop(0, steps // 2, pair, best)

    columns = (SEQ - 1) * QW
    wait_bytes(out.at[0, :, pl.ds(0, QW)], out_local)
    wait_bytes(x.at[0, :, pl.ds(0, columns)], q_send)
    wait_bytes(x.at[0, :, pl.ds(0, 14 * HEAD_DIM)], kv_send.at[OWN])
    wait_bytes(x.at[0, :, pl.ds(0, 14 * HEAD_DIM)], kv_send.at[CACHE])
    for part in range(2):
        side_copy(OWN, part).wait_send()
        side_copy(CACHE, part).wait_send()

        @pl.when(c < SPANS - 1)
        def _():
            pass_copy(OWN, part).wait_send()

        @pl.when(c >= 1)
        def _():
            side_copy(NEAR, part).wait_send()

        @pl.when((c >= 1) & (c < SPANS - 1))
        def _():
            pass_copy(NEAR, part).wait_send()

        @pl.when(c >= 2)
        def _():
            side_copy(FAR, part).wait_send()

    wait_bytes(out.at[0, :, pl.ds(0, columns)], out_send)
    wait_bytes(out.at[0, :, pl.ds(0, columns)], out_recv)


def on_device(projected, cache_kv, levels, cache_blocks, gate_table):
    cache_rows = cache_kv.reshape(TOK, 2 * KV_WIDTH)
    dma = pltpu.SemaphoreType.DMA
    return pl.pallas_call(
        kernel,
        out_shape=jax.ShapeDtypeStruct((1, TOK, MODEL_WIDTH), jnp.bfloat16),
        in_specs=[
            pl.BlockSpec(memory_space=pl.ANY),
            pl.BlockSpec(memory_space=pl.ANY),
            pl.BlockSpec(memory_space=pltpu.SMEM),
            pl.BlockSpec(memory_space=pltpu.SMEM),
            pl.BlockSpec(memory_space=pltpu.VMEM),
        ],
        out_specs=pl.BlockSpec(memory_space=pl.ANY),
        scratch_shapes=[
            pltpu.VMEM((4, 2, 2, HALF, HEAD_DIM), jnp.bfloat16),
            pltpu.VMEM((4, HEAD_DIM, SPAN_TOKENS), jnp.bfloat16),
            pltpu.VMEM((SEQ, TOK, QW), jnp.bfloat16),
            pltpu.VMEM((QBLOCKS, 2 * HEAD_DIM, BQ), jnp.bfloat16),
            pltpu.VMEM((QBLOCKS, HEAD_DIM, BQ), jnp.float32),
            pltpu.VMEM((QBLOCKS, 8, BQ), jnp.float32),
            pltpu.VMEM((QBLOCKS, 8, BQ), jnp.float32),
            pltpu.VMEM((SPAN_TOKENS, BQ), jnp.float32),
            pltpu.VMEM((SPAN_TOKENS, BQ), jnp.float32),
            pltpu.VMEM((QBLOCKS, BQ, HEAD_DIM), jnp.bfloat16),
            pltpu.VMEM((8, QW), jnp.float32),
            dma((2,)), dma((2, 2)), dma((3,)), dma((4, 2)), dma((4, 2)), dma((2, 2)), dma((2, 2)),
            dma, dma((4,)), dma, dma, dma,
        ],
        compiler_params=pltpu.CompilerParams(
            collective_id=0, has_side_effects=True, vmem_limit_bytes=50 * 2**20
        ),
    )(projected, cache_rows, levels, cache_blocks, gate_table)


def solution(mesh):
    placed = (P("span", "seq", None), P("seq", None, None), P("span"), P("span"), P(None, "seq"))
    return jax.shard_map(
        on_device, mesh=mesh, in_specs=placed, out_specs=P("span", "seq", None), check_vma=False
    )
```

```python
import functools

import jax
import jax.numpy as jnp
from jax import lax
from jax.experimental import pallas as pl
from jax.experimental.pallas import tpu as pltpu
from jax.sharding import PartitionSpec as P

MODEL_WIDTH = 6144
HEAD_DIM = 128
KV_WIDTH = 1024
SPANS = 8
SEQ = 16
TOK = 128
HEADS = 3
QW = HEADS * HEAD_DIM
SPAN_TOKENS = 2048
HALF = SPAN_TOKENS // 2
CHUNK = 512
BQ = 512
QBLOCKS = 12
SUB = 256
NEGATIVE = -1e30
MASKED = 1e30
SCALE = HEAD_DIM ** -0.5 * 1.4426950408889634
OWN, CACHE, NEAR, FAR = range(4)
MESH = pl.DeviceIdType.MESH

CACHE_SENT = 11
Q_SENT = ((1, 1, 1), (1, 2, 1), (3, 1, 2), (3, 2, 2), (5, 3, 0), (7, 3, 1), (9, 3, 2))
CACHE_STEP = 19
NEAR_STEPS = (6, 8)
FAR_STEPS = (17, 21)
EARLY_BLOCKS = 9


def kernel(
    x, cache, levels, blocks, gate, out,
    kv, vt, qin, qt, acc, top, total, s0, s1, stage, gates, gate_rows,
    kv_send, kv_recv, local_sem, side_send, side_recv, pass_send, pass_recv,
    q_send, q_recv, out_send, out_recv, out_local, gate_sem,
):
    c = lax.axis_index("span")
    s = lax.axis_index("seq")
    chip = s // 2
    core = s % 2
    xlo = chip // 4
    y = chip % 4
    group = s // 4
    limit = blocks[0]
    windows = jnp.minimum(c, 2)
    ways = jnp.where(c >= 2, 2, 1)
    steps = 2 * QBLOCKS + QBLOCKS * windows
    closing = QBLOCKS + QBLOCKS * jnp.minimum(c, 1)
    beside = {"span": c, "seq": 2 * chip + (1 - core)}
    flip = c // (SPANS // 2)
    slot = (s + SEQ // 2 * flip) % SEQ
    head_group = (chip + SEQ // 4 * flip) % (SEQ // 2)
    across = (s + SEQ // 2) % SEQ
    after = {"span": jnp.minimum(c + 1, SPANS - 1), "seq": jnp.where(c == SPANS // 2 - 1, across, s)}
    before = {"span": jnp.maximum(c - 1, 0), "seq": jnp.where(c == SPANS // 2, across, s)}

    barrier = pltpu.get_barrier_semaphore()
    for d in range(1, SEQ):
        pl.semaphore_signal(barrier, inc=1, device_id={"span": c, "seq": (s + d) % SEQ}, device_id_type=MESH)

    @pl.when(c > 0)
    def _():
        pl.semaphore_signal(barrier, inc=1, device_id=before, device_id_type=MESH)

    @pl.when(c < SPANS - 1)
    def _():
        pl.semaphore_signal(barrier, inc=1, device_id=after, device_id_type=MESH)

    def clear(i, unused):
        acc[i] = jnp.zeros((HEAD_DIM, BQ), jnp.float32)
        total[i] = jnp.zeros((8, BQ), jnp.float32)
        top[i] = jnp.full((8, BQ), NEGATIVE, jnp.float32)
        return unused

    lax.fori_loop(0, QBLOCKS, clear, 0)
    pl.semaphore_wait(barrier, SEQ - 1 + jnp.where(c > 0, 1, 0) + jnp.where(c < SPANS - 1, 1, 0))

    def source(stream, which, head):
        if stream == OWN:
            return x.at[0, :, pl.ds(pl.multiple_of(MODEL_WIDTH + KV_WIDTH * which + HEAD_DIM * head, 128), HEAD_DIM)]
        return cache.at[:, pl.ds(pl.multiple_of(KV_WIDTH * which + HEAD_DIM * head, 128), HEAD_DIM)]

    def send_kv(stream):
        piece = pl.ds(pl.multiple_of(TOK * chip, TOK), TOK)
        for dx, dy in ((0, 1), (0, 3), (0, 2), (1, 0), (1, 1), (1, 3), (1, 2)):
            there = ((xlo + dx) % 2) * 4 + (y + dy) % 4
            for which in range(2):
                pltpu.make_async_remote_copy(
                    src_ref=source(stream, which, (there + SEQ // 4 * flip) % (SEQ // 2)),
                    dst_ref=kv.at[stream, core, which, piece],
                    send_sem=kv_send.at[stream],
                    recv_sem=kv_recv.at[stream, xlo],
                    device_id={"span": c, "seq": 2 * there + core},
                    device_id_type=MESH,
                ).start()
        for which in range(2):
            pltpu.make_async_copy(source(stream, which, head_group), kv.at[stream, core, which, piece], local_sem.at[stream]).start()

    def group_at(turn):
        return ((group // 2 + turn // 2) % 2) * 2 + (group % 2 + turn % 2) % 2

    def send_q(turn, head):
        for e in range(4):
            there = 4 * group_at(turn) + (s % 4 + e) % 4
            if turn == 0 and e == 0:
                continue
            pltpu.make_async_remote_copy(
                src_ref=x.at[0, :, pl.ds(pl.multiple_of(QW * ((there + SEQ // 2 * flip) % SEQ) + HEAD_DIM * head, 128), HEAD_DIM)],
                dst_ref=qin.at[s, :, pl.ds(HEAD_DIM * head, HEAD_DIM)],
                send_sem=q_send,
                recv_sem=q_recv.at[group, head],
                device_id={"span": c, "seq": there},
                device_id_type=MESH,
            ).start()

    gate_copy = pltpu.make_async_remote_copy(
        src_ref=gate, dst_ref=gate_rows, send_sem=gate_sem.at[0], recv_sem=gate_sem.at[1],
        device_id={"span": c, "seq": across}, device_id_type=MESH,
    )

    @pl.when(flip == 0)
    def _():
        pltpu.make_async_copy(gate, gate_rows, local_sem.at[3]).start()

    @pl.when(flip == 1)
    def _():
        gate_copy.start()

    send_kv(OWN)
    pltpu.make_async_copy(x.at[0, :, pl.ds(pl.multiple_of(QW * slot, 128), QW)], qin.at[s], local_sem.at[2]).start()
    send_q(0, 0)

    def wait_bytes(ref, sem):
        pltpu.make_async_copy(ref, ref, sem).wait()

    def half_rows(part):
        return pl.ds(pl.multiple_of(CHUNK * part, CHUNK), CHUNK)

    def side_copy(stream, part):
        piece = kv.at[stream, core, :, half_rows(part)]
        return pltpu.make_async_remote_copy(
            src_ref=piece, dst_ref=piece, send_sem=side_send.at[stream, part], recv_sem=side_recv.at[stream, part],
            device_id=beside, device_id_type=MESH,
        )

    def pass_copy(stream, part):
        return pltpu.make_async_remote_copy(
            src_ref=kv.at[stream, core, :, half_rows(part)],
            dst_ref=kv.at[FAR if stream == NEAR else NEAR, core, :, half_rows(part)],
            send_sem=pass_send.at[stream // 2, part], recv_sem=pass_recv.at[stream // 2, part],
            device_id=after, device_id_type=MESH,
        )

    def take_kv(stream, first):
        part = xlo if first else 1 - xlo
        if first:
            wait_bytes(kv.at[stream, core, :, pl.ds(0, TOK)], local_sem.at[stream])
        rows = 3 * TOK if first else 4 * TOK
        wait_bytes(kv.at[stream, core, :, pl.ds(0, rows)], kv_recv.at[stream, part])
        side_copy(stream, part).start()
        if stream == OWN:
            @pl.when(c < SPANS - 1)
            def _():
                pass_copy(OWN, part).start()

    def take_window(stream, first):
        part = xlo if first else 1 - xlo
        wait_bytes(kv.at[stream, core, :, pl.ds(0, CHUNK)], pass_recv.at[0 if stream == NEAR else 1, part])
        side_copy(stream, part).start()
        if stream == NEAR:
            @pl.when(c < SPANS - 1)
            def _():
                pass_copy(NEAR, part).start()

    def take_side(stream):
        for part in range(2):
            wait_bytes(kv.at[stream, 1 - core, :, pl.ds(0, CHUNK)], side_recv.at[stream, part])
        for p in range(2):
            for b in range(0, HALF, 512):
                values = kv[stream, p, 1, pl.ds(b, 512), :]
                vt[stream, :, pl.ds(p * HALF + b, 512)] = jnp.transpose(values)

    def turn_of(i):
        middle = (i >= HEADS) & (i < EARLY_BLOCKS)
        turn = jnp.where(i < HEADS, 0, jnp.where(middle, 1 + (i - HEADS) % 2, 3))
        head = jnp.where(i < HEADS, i, jnp.where(middle, (i - HEADS) // 2, i - EARLY_BLOCKS))
        return turn, head

    def take_q(i):
        turn, h = turn_of(i)
        g = group_at(turn)

        @pl.when(i == 0)
        def _():
            wait_bytes(qin.at[0], local_sem.at[2])

        @pl.when(i < HEADS)
        def _():
            wait_bytes(qin.at[pl.ds(0, 3), :, pl.ds(0, HEAD_DIM)], q_recv.at[g, h])

        @pl.when(i >= HEADS)
        def _():
            wait_bytes(qin.at[pl.ds(0, 4), :, pl.ds(0, HEAD_DIM)], q_recv.at[g, h])

        rows = qin[pl.ds(4 * g, 4), :, pl.ds(pl.multiple_of(h * HEAD_DIM, 128), HEAD_DIM)].reshape(BQ, HEAD_DIM)
        scaled = jnp.transpose(rows.astype(jnp.float32) * SCALE)
        high = scaled.astype(jnp.bfloat16)
        qt[i, pl.ds(0, 128), :] = high
        qt[i, pl.ds(128, 128), :] = (scaled - high.astype(jnp.float32)).astype(jnp.bfloat16)

    def place(t):
        late = t - closing
        once = 2 * EARLY_BLOCKS
        rest = QBLOCKS - EARLY_BLOCKS
        near = (c >= 1) & (((t >= EARLY_BLOCKS) & (t < once)) | (t >= once + rest))
        skipped = jnp.where((c >= 1) & (t >= EARLY_BLOCKS), jnp.where(t >= once + rest, QBLOCKS, EARLY_BLOCKS), 0)
        stream = jnp.where(late < 0, jnp.where(near, NEAR, OWN), jnp.where(late % ways == 0, CACHE, FAR))
        block = jnp.where(late < 0, t - skipped, QBLOCKS - 1 - late // ways)
        return stream, block

    def masked(stream, p, piece):
        return jnp.where((stream == CACHE) & (2 * piece + p >= limit), MASKED, 0.0).astype(jnp.float32)

    def score_part(stream, queries, into, ch, best):
        p, start = divmod(ch * SUB, HALF)
        keys = kv[stream, p, 0, pl.ds(start, SUB), :]
        part = jnp.dot(jnp.concatenate([keys, keys], axis=1), queries, preferred_element_type=jnp.float32)
        into[pl.ds(ch * SUB, SUB), :] = part
        for b in range(SUB // TOK):
            here = jnp.max(part[b * TOK:(b + 1) * TOK].reshape(TOK // 8, 8, BQ), axis=0)
            here = here - masked(stream, p, (start + b * TOK) // TOK)
            best = here if best is None else jnp.maximum(best, here)
        return best

    def raised(block, best):
        old = top[block, 0:1, :]
        return old, jnp.maximum(old, jnp.max(best, axis=0, keepdims=True))

    def arrivals(t):
        @pl.when((t < EARLY_BLOCKS) | ((c == 0) & (t < QBLOCKS)))
        def _():
            take_q(t)

        @pl.when((c >= 1) & (t >= 2 * EARLY_BLOCKS) & (t < EARLY_BLOCKS + QBLOCKS))
        def _():
            take_q(t - EARLY_BLOCKS)

        for at, turn, head in Q_SENT:
            @pl.when(t == at)
            def _(turn=turn, head=head):
                send_q(turn, head)

        @pl.when(t == CACHE_SENT)
        def _():
            send_kv(CACHE)

        @pl.when(t == jnp.where(c == 0, QBLOCKS - 1, CACHE_STEP))
        def _():
            take_kv(CACHE, True)
            take_kv(CACHE, False)

        for which, at in enumerate(NEAR_STEPS):
            @pl.when((t == at) & (c >= 1))
            def _(which=which):
                take_window(NEAR, which == 0)

        for which, at in enumerate(FAR_STEPS):
            @pl.when((t == at) & (c >= 2))
            def _(which=which):
                take_window(FAR, which == 0)

        @pl.when((t == EARLY_BLOCKS) & (c >= 1))
        def _():
            take_side(NEAR)

        @pl.when(t == closing)
        def _():
            take_side(CACHE)

        @pl.when((t == closing + 1) & (c >= 2))
        def _():
            take_side(FAR)

    def finish(block):
        summed = acc[block]
        whole = jnp.sum(total[block], axis=0, keepdims=True)
        square = jnp.mean(summed * summed, axis=0, keepdims=True)
        normed = summed * lax.rsqrt(square + 1e-06 * (whole * whole))
        turn, h = turn_of(block)
        g = group_at(turn)
        row = gates[0:1, pl.ds(pl.multiple_of(h * HEAD_DIM, 128), HEAD_DIM)]
        stage[block] = (jnp.transpose(normed) * row).astype(jnp.bfloat16)
        wanted = out.at[0, :, pl.ds(pl.multiple_of((HEADS * slot + h) * HEAD_DIM, 128), HEAD_DIM)]
        for e in range(4):
            there = 4 * g + e
            held = stage.at[block, pl.ds(e * TOK, TOK)]

            @pl.when(there == s)
            def _():
                pltpu.make_async_copy(held, wanted, out_local).start()

            @pl.when(there != s)
            def _():
                pltpu.make_async_remote_copy(
                    src_ref=held, dst_ref=wanted, send_sem=out_send, recv_sem=out_recv,
                    device_id={"span": c, "seq": there}, device_id_type=MESH,
                ).start()

    def step(t, now, later, best):
        old, new = best
        stream, block = place(t)
        top[block, 0:1, :] = new

        @pl.when(t + 1 < steps)
        def _():
            arrivals(t + 1)

        next_stream, next_block = place(jnp.minimum(t + 1, steps - 1))
        queries = qt[next_block]
        factor = jnp.exp2(old - new)
        best = None
        update = None
        sums = None
        for ch in range(SPAN_TOKENS // SUB):
            best = score_part(next_stream, queries, later, ch, best)
            p, start = divmod(ch * SUB, HALF)
            rounded = []
            for b in range(SUB // TOK):
                shift = new + masked(stream, p, (start + b * TOK) // TOK)
                weights = jnp.exp2(now[pl.ds(ch * SUB + b * TOK, TOK), :] - shift)
                part = jnp.sum(weights.reshape(TOK // 8, 8, BQ), axis=0)
                sums = part if sums is None else sums + part
                rounded.append(weights.astype(jnp.bfloat16))
            product = jnp.dot(
                vt[stream, :, pl.ds(ch * SUB, SUB)], jnp.concatenate(rounded, axis=0), preferred_element_type=jnp.float32
            )
            update = product if update is None else update + product
        acc[block] = acc[block] * factor + update
        total[block] = total[block] * factor + sums

        @pl.when((t >= closing) & ((t - closing) % ways == ways - 1))
        def _():
            finish(block)

        return raised(next_block, best)

    @pl.when(flip == 0)
    def _():
        pltpu.make_async_copy(gate, gate_rows, local_sem.at[3]).wait()

    @pl.when(flip == 1)
    def _():
        gate_copy.wait()

    level_rows = lax.broadcasted_iota(jnp.int32, gate_rows.shape, 0)
    chosen = jnp.sum(jnp.where(level_rows == levels[0], gate_rows[...], 0.0), axis=0, keepdims=True)
    gates[...] = jnp.broadcast_to(chosen, gates.shape)

    take_kv(OWN, True)
    send_q(0, 1)
    send_q(0, 2)
    take_kv(OWN, False)
    send_q(1, 0)
    send_q(2, 0)
    take_q(jnp.int32(0))
    take_side(OWN)
    best = None
    for ch in range(SPAN_TOKENS // SUB):
        best = score_part(OWN, qt[0], s0, ch, best)
    best = raised(0, best)

    def pair(i, best):
        best = step(2 * i, s0, s1, best)
        return step(2 * i + 1, s1, s0, best)

    lax.fori_loop(0, steps // 2, pair, best)

    columns = (SEQ - 1) * QW
    wait_bytes(out.at[0, :, pl.ds(0, QW)], out_local)
    wait_bytes(x.at[0, :, pl.ds(0, columns)], q_send)
    wait_bytes(x.at[0, :, pl.ds(0, 14 * HEAD_DIM)], kv_send.at[OWN])
    wait_bytes(x.at[0, :, pl.ds(0, 14 * HEAD_DIM)], kv_send.at[CACHE])
    for part in range(2):
        side_copy(OWN, part).wait_send()
        side_copy(CACHE, part).wait_send()

        @pl.when(c < SPANS - 1)
        def _():
            pass_copy(OWN, part).wait_send()

        @pl.when(c >= 1)
        def _():
            side_copy(NEAR, part).wait_send()

        @pl.when((c >= 1) & (c < SPANS - 1))
        def _():
            pass_copy(NEAR, part).wait_send()

        @pl.when(c >= 2)
        def _():
            side_copy(FAR, part).wait_send()

    wait_bytes(out.at[0, :, pl.ds(0, columns)], out_send)
    wait_bytes(out.at[0, :, pl.ds(0, columns)], out_recv)


def on_device(projected, cache_kv, levels, cache_blocks, gate_table):
    cache_rows = cache_kv.reshape(TOK, 2 * KV_WIDTH)
    dma = pltpu.SemaphoreType.DMA
    return pl.pallas_call(
        kernel,
        out_shape=jax.ShapeDtypeStruct((1, TOK, MODEL_WIDTH), jnp.bfloat16),
        in_specs=[
            pl.BlockSpec(memory_space=pl.ANY),
            pl.BlockSpec(memory_space=pl.ANY),
            pl.BlockSpec(memory_space=pltpu.SMEM),
            pl.BlockSpec(memory_space=pltpu.SMEM),
            pl.BlockSpec(memory_space=pl.ANY),
        ],
        out_specs=pl.BlockSpec(memory_space=pl.ANY),
        scratch_shapes=[
            pltpu.VMEM((4, 2, 2, HALF, HEAD_DIM), jnp.bfloat16),
            pltpu.VMEM((4, HEAD_DIM, SPAN_TOKENS), jnp.bfloat16),
            pltpu.VMEM((SEQ, TOK, QW), jnp.bfloat16),
            pltpu.VMEM((QBLOCKS, 2 * HEAD_DIM, BQ), jnp.bfloat16),
            pltpu.VMEM((QBLOCKS, HEAD_DIM, BQ), jnp.float32),
            pltpu.VMEM((QBLOCKS, 8, BQ), jnp.float32),
            pltpu.VMEM((QBLOCKS, 8, BQ), jnp.float32),
            pltpu.VMEM((SPAN_TOKENS, BQ), jnp.float32),
            pltpu.VMEM((SPAN_TOKENS, BQ), jnp.float32),
            pltpu.VMEM((QBLOCKS, BQ, HEAD_DIM), jnp.bfloat16),
            pltpu.VMEM((8, QW), jnp.float32),
            pltpu.VMEM((16, QW), jnp.float32),
            dma((2,)), dma((2, 2)), dma((4,)), dma((4, 2)), dma((4, 2)), dma((2, 2)), dma((2, 2)),
            dma, dma((4, 3)), dma, dma, dma, dma((2,)),
        ],
        compiler_params=pltpu.CompilerParams(
            collective_id=0, has_side_effects=True, vmem_limit_bytes=50 * 2**20
        ),
    )(projected, cache_rows, levels, cache_blocks, gate_table)


def solution(mesh):
    placed = (P("span", "seq", None), P("seq", None, None), P("span"), P("span"), P(None, "seq"))
    return jax.shard_map(
        on_device, mesh=mesh, in_specs=placed, out_specs=P("span", "seq", None), check_vma=False
    )
```

```python
import functools

import jax
import jax.numpy as jnp
from jax import lax
from jax.experimental import pallas as pl
from jax.experimental.pallas import tpu as pltpu
from jax.sharding import PartitionSpec as P

MODEL_WIDTH = 6144
HEAD_DIM = 128
KV_WIDTH = 1024
SPANS = 8
SEQ = 16
TOK = 128
HEADS = 3
QW = HEADS * HEAD_DIM
SPAN_TOKENS = 2048
HALF = SPAN_TOKENS // 2
CHUNK = 512
BQ = 512
QBLOCKS = 12
SUB = 256
NEGATIVE = -1e30
MASKED = 1e30
SCALE = HEAD_DIM ** -0.5 * 1.4426950408889634
OWN, CACHE, NEAR, FAR = range(4)
MESH = pl.DeviceIdType.MESH

CACHE_SENT = 11
Q_SENT = ((1, 1, 1), (1, 2, 1), (3, 1, 2), (3, 2, 2), (5, 3, 0), (7, 3, 1), (9, 3, 2))
CACHE_STEP = 19
NEAR_STEPS = (6, 8)
FAR_STEPS = (17, 21)
EARLY_BLOCKS = 9


def kernel(
    x, cache, levels, blocks, gate, out,
    kv, vt, qin, qt, acc, top, total, s0, s1, stage, gates, gate_rows,
    kv_send, kv_recv, local_sem, side_send, side_recv, pass_send, pass_recv,
    q_send, q_recv, out_send, out_recv, out_local, gate_sem,
):
    c = lax.axis_index("span")
    s = lax.axis_index("seq")
    chip = s // 2
    core = s % 2
    xlo = chip // 4
    y = chip % 4
    group = s // 4
    limit = blocks[0]
    windows = jnp.minimum(c, 2)
    ways = jnp.where(c >= 2, 2, 1)
    steps = 2 * QBLOCKS + QBLOCKS * windows
    closing = QBLOCKS + QBLOCKS * jnp.minimum(c, 1)
    beside = {"span": c, "seq": 2 * chip + (1 - core)}
    flip = c // (SPANS // 2)
    slot = (s + SEQ // 2 * flip) % SEQ
    head_group = (chip + SEQ // 4 * flip) % (SEQ // 2)
    across = (s + SEQ // 2) % SEQ
    after = {"span": jnp.minimum(c + 1, SPANS - 1), "seq": jnp.where(c == SPANS // 2 - 1, across, s)}
    before = {"span": jnp.maximum(c - 1, 0), "seq": jnp.where(c == SPANS // 2, across, s)}

    barrier = pltpu.get_barrier_semaphore()
    for d in range(1, SEQ):
        pl.semaphore_signal(barrier, inc=1, device_id={"span": c, "seq": (s + d) % SEQ}, device_id_type=MESH)

    @pl.when(c > 0)
    def _():
        pl.semaphore_signal(barrier, inc=1, device_id=before, device_id_type=MESH)

    @pl.when(c < SPANS - 1)
    def _():
        pl.semaphore_signal(barrier, inc=1, device_id=after, device_id_type=MESH)

    def source(stream, which, head):
        if stream == OWN:
            return x.at[0, :, pl.ds(pl.multiple_of(MODEL_WIDTH + KV_WIDTH * which + HEAD_DIM * head, 128), HEAD_DIM)]
        return cache.at[:, pl.ds(pl.multiple_of(KV_WIDTH * which + HEAD_DIM * head, 128), HEAD_DIM)]

    piece = pl.ds(pl.multiple_of(TOK * chip, TOK), TOK)

    for stream in (OWN, CACHE):
        for which in range(2):
            pltpu.make_async_copy(source(stream, which, head_group), kv.at[stream, core, which, piece], local_sem.at[stream]).start()
    pltpu.make_async_copy(x.at[0, :, pl.ds(pl.multiple_of(QW * slot, 128), QW)], qin.at[s], local_sem.at[2]).start()

    def clear(i, unused):
        acc[i] = jnp.zeros((HEAD_DIM, BQ), jnp.float32)
        total[i] = jnp.zeros((8, BQ), jnp.float32)
        top[i] = jnp.full((8, BQ), NEGATIVE, jnp.float32)
        return unused

    lax.fori_loop(0, QBLOCKS, clear, 0)
    pl.semaphore_wait(barrier, SEQ - 1 + jnp.where(c > 0, 1, 0) + jnp.where(c < SPANS - 1, 1, 0))

    def send_kv(stream):
        for dx, dy in ((0, 1), (0, 3), (0, 2), (1, 0), (1, 1), (1, 3), (1, 2)):
            there = ((xlo + dx) % 2) * 4 + (y + dy) % 4
            for which in range(2):
                pltpu.make_async_remote_copy(
                    src_ref=source(stream, which, (there + SEQ // 4 * flip) % (SEQ // 2)),
                    dst_ref=kv.at[stream, core, which, piece],
                    send_sem=kv_send.at[stream],
                    recv_sem=kv_recv.at[stream, xlo],
                    device_id={"span": c, "seq": 2 * there + core},
                    device_id_type=MESH,
                ).start()

    def group_at(turn):
        return ((group // 2 + turn // 2) % 2) * 2 + (group % 2 + turn % 2) % 2

    def send_q(turn, head):
        for e in range(4):
            there = 4 * group_at(turn) + (s % 4 + e) % 4
            if turn == 0 and e == 0:
                continue
            pltpu.make_async_remote_copy(
                src_ref=x.at[0, :, pl.ds(pl.multiple_of(QW * ((there + SEQ // 2 * flip) % SEQ) + HEAD_DIM * head, 128), HEAD_DIM)],
                dst_ref=qin.at[s, :, pl.ds(HEAD_DIM * head, HEAD_DIM)],
                send_sem=q_send,
                recv_sem=q_recv.at[group, head],
                device_id={"span": c, "seq": there},
                device_id_type=MESH,
            ).start()

    gate_copy = pltpu.make_async_remote_copy(
        src_ref=gate, dst_ref=gate_rows, send_sem=gate_sem.at[0], recv_sem=gate_sem.at[1],
        device_id={"span": c, "seq": across}, device_id_type=MESH,
    )

    @pl.when(flip == 0)
    def _():
        pltpu.make_async_copy(gate, gate_rows, local_sem.at[3]).start()

    @pl.when(flip == 1)
    def _():
        gate_copy.start()

    send_kv(OWN)
    send_q(0, 0)

    def wait_bytes(ref, sem):
        pltpu.make_async_copy(ref, ref, sem).wait()

    def half_rows(part):
        return pl.ds(pl.multiple_of(CHUNK * part, CHUNK), CHUNK)

    def side_copy(stream, part):
        piece = kv.at[stream, core, :, half_rows(part)]
        return pltpu.make_async_remote_copy(
            src_ref=piece, dst_ref=piece, send_sem=side_send.at[stream, part], recv_sem=side_recv.at[stream, part],
            device_id=beside, device_id_type=MESH,
        )

    def pass_copy(stream, part):
        return pltpu.make_async_remote_copy(
            src_ref=kv.at[stream, core, :, half_rows(part)],
            dst_ref=kv.at[FAR if stream == NEAR else NEAR, core, :, half_rows(part)],
            send_sem=pass_send.at[stream // 2, part], recv_sem=pass_recv.at[stream // 2, part],
            device_id=after, device_id_type=MESH,
        )

    def take_kv(stream, first):
        part = xlo if first else 1 - xlo
        if first:
            wait_bytes(kv.at[stream, core, :, pl.ds(0, TOK)], local_sem.at[stream])
        rows = 3 * TOK if first else 4 * TOK
        wait_bytes(kv.at[stream, core, :, pl.ds(0, rows)], kv_recv.at[stream, part])
        side_copy(stream, part).start()
        if stream == OWN:
            @pl.when(c < SPANS - 1)
            def _():
                pass_copy(OWN, part).start()

    def take_window(stream, first):
        part = xlo if first else 1 - xlo
        wait_bytes(kv.at[stream, core, :, pl.ds(0, CHUNK)], pass_recv.at[0 if stream == NEAR else 1, part])
        side_copy(stream, part).start()
        if stream == NEAR:
            @pl.when(c < SPANS - 1)
            def _():
                pass_copy(NEAR, part).start()

    def turn_values(stream, p):
        for b in range(0, HALF, 512):
            columns = pl.ds(pl.multiple_of(p * HALF + b, 512), 512)
            vt[stream, :, columns] = jnp.transpose(kv[stream, p, 1, pl.ds(b, 512), :])

    def take_side(stream):
        turn_values(stream, core)
        for part in range(2):
            wait_bytes(kv.at[stream, 1 - core, :, pl.ds(0, CHUNK)], side_recv.at[stream, part])
        turn_values(stream, 1 - core)

    def turn_of(i):
        middle = (i >= HEADS) & (i < EARLY_BLOCKS)
        turn = jnp.where(i < HEADS, 0, jnp.where(middle, 1 + (i - HEADS) % 2, 3))
        head = jnp.where(i < HEADS, i, jnp.where(middle, (i - HEADS) // 2, i - EARLY_BLOCKS))
        return turn, head

    def take_q(i):
        turn, h = turn_of(i)
        g = group_at(turn)

        @pl.when(i == 0)
        def _():
            wait_bytes(qin.at[0], local_sem.at[2])

        @pl.when(i < HEADS)
        def _():
            wait_bytes(qin.at[pl.ds(0, 3), :, pl.ds(0, HEAD_DIM)], q_recv.at[g, h])

        @pl.when(i >= HEADS)
        def _():
            wait_bytes(qin.at[pl.ds(0, 4), :, pl.ds(0, HEAD_DIM)], q_recv.at[g, h])

        rows = qin[pl.ds(4 * g, 4), :, pl.ds(pl.multiple_of(h * HEAD_DIM, 128), HEAD_DIM)].reshape(BQ, HEAD_DIM)
        scaled = jnp.transpose(rows).astype(jnp.float32) * SCALE
        high = scaled.astype(jnp.bfloat16)
        qt[i, pl.ds(0, 128), :] = high
        qt[i, pl.ds(128, 128), :] = (scaled - high.astype(jnp.float32)).astype(jnp.bfloat16)

    def place(t):
        late = t - closing
        once = 2 * EARLY_BLOCKS
        rest = QBLOCKS - EARLY_BLOCKS
        near = (c >= 1) & (((t >= EARLY_BLOCKS) & (t < once)) | (t >= once + rest))
        skipped = jnp.where((c >= 1) & (t >= EARLY_BLOCKS), jnp.where(t >= once + rest, QBLOCKS, EARLY_BLOCKS), 0)
        stream = jnp.where(late < 0, jnp.where(near, NEAR, OWN), jnp.where(late % ways == 0, CACHE, FAR))
        block = jnp.where(late < 0, t - skipped, QBLOCKS - 1 - late // ways)
        return stream, block

    def masked(stream, p, piece):
        return jnp.where((stream == CACHE) & (2 * piece + p >= limit), MASKED, 0.0).astype(jnp.float32)

    def score_part(stream, queries, into, ch, best):
        p, start = divmod(ch * SUB, HALF)
        keys = kv[stream, p, 0, pl.ds(start, SUB), :]
        part = jnp.dot(jnp.concatenate([keys, keys], axis=1), queries, preferred_element_type=jnp.float32)
        into[pl.ds(ch * SUB, SUB), :] = part
        for b in range(SUB // TOK):
            here = jnp.max(part[b * TOK:(b + 1) * TOK].reshape(TOK // 8, 8, BQ), axis=0)
            here = here - masked(stream, p, (start + b * TOK) // TOK)
            best = here if best is None else jnp.maximum(best, here)
        return best

    def raised(block, best):
        old = top[block, 0:1, :]
        return old, jnp.maximum(old, jnp.max(best, axis=0, keepdims=True))

    def arrivals(t):
        @pl.when((t < EARLY_BLOCKS) | ((c == 0) & (t < QBLOCKS)))
        def _():
            take_q(t)

        @pl.when((c >= 1) & (t >= 2 * EARLY_BLOCKS) & (t < EARLY_BLOCKS + QBLOCKS))
        def _():
            take_q(t - EARLY_BLOCKS)

        for at, turn, head in Q_SENT:
            @pl.when(t == at)
            def _(turn=turn, head=head):
                send_q(turn, head)

        @pl.when(t == CACHE_SENT)
        def _():
            send_kv(CACHE)

        @pl.when(t == jnp.where(c == 0, QBLOCKS - 1, CACHE_STEP))
        def _():
            take_kv(CACHE, True)
            take_kv(CACHE, False)

        for which, at in enumerate(NEAR_STEPS):
            @pl.when((t == at) & (c >= 1))
            def _(which=which):
                take_window(NEAR, which == 0)

        for which, at in enumerate(FAR_STEPS):
            @pl.when((t == at) & (c >= 2))
            def _(which=which):
                take_window(FAR, which == 0)

        @pl.when((t == EARLY_BLOCKS) & (c >= 1))
        def _():
            take_side(NEAR)

        @pl.when(t == closing)
        def _():
            take_side(CACHE)

        @pl.when((t == closing + 1) & (c >= 2))
        def _():
            take_side(FAR)

    def finish(block):
        summed = acc[block]
        whole = jnp.sum(total[block], axis=0, keepdims=True)
        square = jnp.mean(summed * summed, axis=0, keepdims=True)
        normed = summed * lax.rsqrt(square + 1e-06 * (whole * whole))
        turn, h = turn_of(block)
        g = group_at(turn)
        scale = jnp.concatenate([gates[h]] * (BQ // HEAD_DIM), axis=1)
        stage[block] = jnp.transpose((normed * scale).astype(jnp.bfloat16))
        wanted = out.at[0, :, pl.ds(pl.multiple_of((HEADS * slot + h) * HEAD_DIM, 128), HEAD_DIM)]
        for e in range(4):
            there = 4 * g + e
            held = stage.at[block, pl.ds(e * TOK, TOK)]

            @pl.when(there == s)
            def _():
                pltpu.make_async_copy(held, wanted, out_local).start()

            @pl.when(there != s)
            def _():
                pltpu.make_async_remote_copy(
                    src_ref=held, dst_ref=wanted, send_sem=out_send, recv_sem=out_recv,
                    device_id={"span": c, "seq": there}, device_id_type=MESH,
                ).start()

    def step(t, now, later, best, last=False):
        old, new = best
        stream, block = place(t)
        top[block, 0:1, :] = new

        if not last:
            arrivals(t + 1)
            next_stream, next_block = place(t + 1)
            queries = qt[next_block]
        factor = jnp.exp2(old - new)
        best = None
        update = None
        sums = None
        for ch in range(SPAN_TOKENS // SUB):
            if not last:
                best = score_part(next_stream, queries, later, ch, best)
            p, start = divmod(ch * SUB, HALF)
            rounded = []
            for b in range(SUB // TOK):
                shift = new + masked(stream, p, (start + b * TOK) // TOK)
                weights = jnp.exp2(now[pl.ds(ch * SUB + b * TOK, TOK), :] - shift)
                part = jnp.sum(weights.reshape(TOK // 8, 8, BQ), axis=0)
                sums = part if sums is None else sums + part
                rounded.append(weights.astype(jnp.bfloat16))
            product = jnp.dot(
                vt[stream, :, pl.ds(ch * SUB, SUB)], jnp.concatenate(rounded, axis=0), preferred_element_type=jnp.float32
            )
            update = product if update is None else update + product
        acc[block] = acc[block] * factor + update
        total[block] = total[block] * factor + sums

        @pl.when((t >= closing) & ((t - closing) % ways == ways - 1))
        def _():
            finish(block)

        return None if last else raised(next_block, best)

    @pl.when(flip == 0)
    def _():
        pltpu.make_async_copy(gate, gate_rows, local_sem.at[3]).wait()

    @pl.when(flip == 1)
    def _():
        gate_copy.wait()

    level_rows = lax.broadcasted_iota(jnp.int32, gate_rows.shape, 0)
    chosen = jnp.sum(jnp.where(level_rows == levels[0], gate_rows[...], 0.0), axis=0, keepdims=True)
    for h in range(HEADS):
        gates[h] = jnp.transpose(jnp.broadcast_to(chosen[:, h * HEAD_DIM:(h + 1) * HEAD_DIM], (HEAD_DIM, HEAD_DIM)))

    take_kv(OWN, True)
    send_q(0, 1)
    send_q(0, 2)
    take_kv(OWN, False)
    send_q(1, 0)
    send_q(2, 0)
    take_q(jnp.int32(0))
    take_side(OWN)
    best = None
    for ch in range(SPAN_TOKENS // SUB):
        best = score_part(OWN, qt[0], s0, ch, best)
    best = raised(0, best)

    def pair(i, best):
        best = step(2 * i, s0, s1, best)
        return step(2 * i + 1, s1, s0, best)

    best = lax.fori_loop(0, steps // 2 - 1, pair, best)
    best = step(steps - 2, s0, s1, best)
    step(steps - 1, s1, s0, best, last=True)

    columns = (SEQ - 1) * QW
    wait_bytes(out.at[0, :, pl.ds(0, QW)], out_local)
    wait_bytes(x.at[0, :, pl.ds(0, columns)], q_send)
    wait_bytes(x.at[0, :, pl.ds(0, 14 * HEAD_DIM)], kv_send.at[OWN])
    wait_bytes(x.at[0, :, pl.ds(0, 14 * HEAD_DIM)], kv_send.at[CACHE])
    for part in range(2):
        side_copy(OWN, part).wait_send()
        side_copy(CACHE, part).wait_send()

        @pl.when(c < SPANS - 1)
        def _():
            pass_copy(OWN, part).wait_send()

        @pl.when(c >= 1)
        def _():
            side_copy(NEAR, part).wait_send()

        @pl.when((c >= 1) & (c < SPANS - 1))
        def _():
            pass_copy(NEAR, part).wait_send()

        @pl.when(c >= 2)
        def _():
            side_copy(FAR, part).wait_send()

    wait_bytes(out.at[0, :, pl.ds(0, columns)], out_send)
    wait_bytes(out.at[0, :, pl.ds(0, columns)], out_recv)


def on_device(projected, cache_kv, levels, cache_blocks, gate_table):
    cache_rows = cache_kv.reshape(TOK, 2 * KV_WIDTH)
    dma = pltpu.SemaphoreType.DMA
    return pl.pallas_call(
        kernel,
        out_shape=jax.ShapeDtypeStruct((1, TOK, MODEL_WIDTH), jnp.bfloat16),
        in_specs=[
            pl.BlockSpec(memory_space=pl.ANY),
            pl.BlockSpec(memory_space=pl.ANY),
            pl.BlockSpec(memory_space=pltpu.SMEM),
            pl.BlockSpec(memory_space=pltpu.SMEM),
            pl.BlockSpec(memory_space=pl.ANY),
        ],
        out_specs=pl.BlockSpec(memory_space=pl.ANY),
        scratch_shapes=[
            pltpu.VMEM((4, 2, 2, HALF, HEAD_DIM), jnp.bfloat16),
            pltpu.VMEM((4, HEAD_DIM, SPAN_TOKENS), jnp.bfloat16),
            pltpu.VMEM((SEQ, TOK, QW), jnp.bfloat16),
            pltpu.VMEM((QBLOCKS, 2 * HEAD_DIM, BQ), jnp.bfloat16),
            pltpu.VMEM((QBLOCKS, HEAD_DIM, BQ), jnp.float32),
            pltpu.VMEM((QBLOCKS, 8, BQ), jnp.float32),
            pltpu.VMEM((QBLOCKS, 8, BQ), jnp.float32),
            pltpu.VMEM((SPAN_TOKENS, BQ), jnp.float32),
            pltpu.VMEM((SPAN_TOKENS, BQ), jnp.float32),
            pltpu.VMEM((QBLOCKS, BQ, HEAD_DIM), jnp.bfloat16),
            pltpu.VMEM((HEADS, HEAD_DIM, HEAD_DIM), jnp.float32),
            pltpu.VMEM((16, QW), jnp.float32),
            dma((2,)), dma((2, 2)), dma((4,)), dma((4, 2)), dma((4, 2)), dma((2, 2)), dma((2, 2)),
            dma, dma((4, 3)), dma, dma, dma, dma((2,)),
        ],
        compiler_params=pltpu.CompilerParams(
            collective_id=0, has_side_effects=True, vmem_limit_bytes=50 * 2**20
        ),
    )(projected, cache_rows, levels, cache_blocks, gate_table)


def solution(mesh):
    placed = (P("span", "seq", None), P("seq", None, None), P("span"), P("span"), P(None, "seq"))
    return jax.shard_map(
        on_device, mesh=mesh, in_specs=placed, out_specs=P("span", "seq", None), check_vma=False
    )
```

```python
import functools

import jax
import jax.numpy as jnp
from jax import lax
from jax.experimental import pallas as pl
from jax.experimental.pallas import tpu as pltpu
from jax.sharding import PartitionSpec as P

MODEL_WIDTH = 6144
HEAD_DIM = 128
KV_WIDTH = 1024
SPANS = 8
SEQ = 16
TOK = 128
HEADS = 3
QW = HEADS * HEAD_DIM
SPAN_TOKENS = 2048
HALF = SPAN_TOKENS // 2
CHUNK = 512
BQ = 512
QBLOCKS = 12
SUB = 256
NEGATIVE = -1e30
MASKED = 1e30
SCALE = HEAD_DIM ** -0.5 * 1.4426950408889634
OWN, CACHE, NEAR, FAR = range(4)
MESH = pl.DeviceIdType.MESH

CACHE_SENT = 11
Q_SENT = ((1, 1, 1), (1, 2, 1), (3, 1, 2), (3, 2, 2), (6, 3, 0), (7, 3, 1), (8, 3, 2))
CACHE_STEP = 19
NEAR_STEPS = (6, 8)
FAR_STEPS = (17, 21)
EARLY_BLOCKS = 9


def kernel(
    x, cache, levels, blocks, gate, out,
    kv, vt, qin, qt, acc, top, total, s0, s1, stage, gates, gate_rows,
    kv_send, kv_recv, local_sem, side_send, side_recv, pass_send, pass_recv,
    q_send, q_recv, out_send, out_recv, out_local, gate_sem,
):
    c = lax.axis_index("span")
    s = lax.axis_index("seq")
    chip = s // 2
    core = s % 2
    xlo = chip // 4
    y = chip % 4
    group = s // 4
    limit = blocks[0]
    windows = jnp.minimum(c, 2)
    ways = jnp.where(c >= 2, 2, 1)
    steps = 2 * QBLOCKS + QBLOCKS * windows
    closing = QBLOCKS + QBLOCKS * jnp.minimum(c, 1)
    beside = {"span": c, "seq": 2 * chip + (1 - core)}
    flip = c // (SPANS // 2)
    slot = (s + SEQ // 2 * flip) % SEQ
    head_group = (chip + SEQ // 4 * flip) % (SEQ // 2)
    across = (s + SEQ // 2) % SEQ
    after = {"span": jnp.minimum(c + 1, SPANS - 1), "seq": jnp.where(c == SPANS // 2 - 1, across, s)}
    before = {"span": jnp.maximum(c - 1, 0), "seq": jnp.where(c == SPANS // 2, across, s)}

    barrier = pltpu.get_barrier_semaphore()
    for d in range(1, SEQ):
        pl.semaphore_signal(barrier, inc=1, device_id={"span": c, "seq": (s + d) % SEQ}, device_id_type=MESH)

    @pl.when(c > 0)
    def _():
        pl.semaphore_signal(barrier, inc=1, device_id=before, device_id_type=MESH)

    @pl.when(c < SPANS - 1)
    def _():
        pl.semaphore_signal(barrier, inc=1, device_id=after, device_id_type=MESH)

    def source(stream, which, head):
        if stream == OWN:
            return x.at[0, :, pl.ds(pl.multiple_of(MODEL_WIDTH + KV_WIDTH * which + HEAD_DIM * head, 128), HEAD_DIM)]
        return cache.at[:, pl.ds(pl.multiple_of(KV_WIDTH * which + HEAD_DIM * head, 128), HEAD_DIM)]

    piece = pl.ds(pl.multiple_of(TOK * chip, TOK), TOK)

    for stream in (OWN, CACHE):
        for which in range(2):
            pltpu.make_async_copy(source(stream, which, head_group), kv.at[stream, core, which, piece], local_sem.at[stream]).start()
    pltpu.make_async_copy(x.at[0, :, pl.ds(pl.multiple_of(QW * slot, 128), QW)], qin.at[s], local_sem.at[2]).start()

    def clear(i, unused):
        acc[i] = jnp.zeros((HEAD_DIM, BQ), jnp.float32)
        total[i] = jnp.zeros((8, BQ), jnp.float32)
        top[i] = jnp.full((8, BQ), NEGATIVE, jnp.float32)
        return unused

    lax.fori_loop(0, QBLOCKS, clear, 0)
    pl.semaphore_wait(barrier, SEQ - 1 + jnp.where(c > 0, 1, 0) + jnp.where(c < SPANS - 1, 1, 0))

    def send_kv(stream):
        for dx, dy in ((0, 1), (0, 3), (0, 2), (1, 0), (1, 1), (1, 3), (1, 2)):
            there = ((xlo + dx) % 2) * 4 + (y + dy) % 4
            for which in range(2):
                pltpu.make_async_remote_copy(
                    src_ref=source(stream, which, (there + SEQ // 4 * flip) % (SEQ // 2)),
                    dst_ref=kv.at[stream, core, which, piece],
                    send_sem=kv_send.at[stream],
                    recv_sem=kv_recv.at[stream, xlo],
                    device_id={"span": c, "seq": 2 * there + core},
                    device_id_type=MESH,
                ).start()

    def group_at(turn):
        return ((group // 2 + turn // 2) % 2) * 2 + (group % 2 + turn % 2) % 2

    def send_q(turn, head):
        for e in range(4):
            there = 4 * group_at(turn) + (s % 4 + e) % 4
            if turn == 0 and e == 0:
                continue
            pltpu.make_async_remote_copy(
                src_ref=x.at[0, :, pl.ds(pl.multiple_of(QW * ((there + SEQ // 2 * flip) % SEQ) + HEAD_DIM * head, 128), HEAD_DIM)],
                dst_ref=qin.at[s, :, pl.ds(HEAD_DIM * head, HEAD_DIM)],
                send_sem=q_send,
                recv_sem=q_recv.at[group, head],
                device_id={"span": c, "seq": there},
                device_id_type=MESH,
            ).start()

    gate_copy = pltpu.make_async_remote_copy(
        src_ref=gate, dst_ref=gate_rows, send_sem=gate_sem.at[0], recv_sem=gate_sem.at[1],
        device_id={"span": c, "seq": across}, device_id_type=MESH,
    )

    @pl.when(flip == 0)
    def _():
        pltpu.make_async_copy(gate, gate_rows, local_sem.at[3]).start()

    @pl.when(flip == 1)
    def _():
        gate_copy.start()

    send_kv(OWN)
    send_q(0, 0)

    def wait_bytes(ref, sem):
        pltpu.make_async_copy(ref, ref, sem).wait()

    def half_rows(part):
        return pl.ds(pl.multiple_of(CHUNK * part, CHUNK), CHUNK)

    def side_copy(stream, part):
        piece = kv.at[stream, core, :, half_rows(part)]
        return pltpu.make_async_remote_copy(
            src_ref=piece, dst_ref=piece, send_sem=side_send.at[stream, part], recv_sem=side_recv.at[stream, part],
            device_id=beside, device_id_type=MESH,
        )

    def pass_copy(stream, part):
        return pltpu.make_async_remote_copy(
            src_ref=kv.at[stream, core, :, half_rows(part)],
            dst_ref=kv.at[FAR if stream == NEAR else NEAR, core, :, half_rows(part)],
            send_sem=pass_send.at[stream // 2, part], recv_sem=pass_recv.at[stream // 2, part],
            device_id=after, device_id_type=MESH,
        )

    def take_kv(stream, first):
        part = xlo if first else 1 - xlo
        if first:
            wait_bytes(kv.at[stream, core, :, pl.ds(0, TOK)], local_sem.at[stream])
        rows = 3 * TOK if first else 4 * TOK
        wait_bytes(kv.at[stream, core, :, pl.ds(0, rows)], kv_recv.at[stream, part])
        side_copy(stream, part).start()
        if stream == OWN:
            @pl.when(c < SPANS - 1)
            def _():
                pass_copy(OWN, part).start()

    def take_window(stream, first):
        part = xlo if first else 1 - xlo
        wait_bytes(kv.at[stream, core, :, pl.ds(0, CHUNK)], pass_recv.at[0 if stream == NEAR else 1, part])
        side_copy(stream, part).start()
        if stream == NEAR:
            @pl.when(c < SPANS - 1)
            def _():
                pass_copy(NEAR, part).start()

    def turn_values(stream, p):
        for b in range(0, HALF, 512):
            columns = pl.ds(pl.multiple_of(p * HALF + b, 512), 512)
            vt[stream, :, columns] = jnp.transpose(kv[stream, p, 1, pl.ds(b, 512), :])

    def take_side(stream):
        turn_values(stream, core)
        for part in range(2):
            wait_bytes(kv.at[stream, 1 - core, :, pl.ds(0, CHUNK)], side_recv.at[stream, part])
        turn_values(stream, 1 - core)

    def turn_of(i):
        middle = (i >= HEADS) & (i < EARLY_BLOCKS)
        turn = jnp.where(i < HEADS, 0, jnp.where(middle, 1 + (i - HEADS) % 2, 3))
        head = jnp.where(i < HEADS, i, jnp.where(middle, (i - HEADS) // 2, i - EARLY_BLOCKS))
        return turn, head

    def take_q(i):
        turn, h = turn_of(i)
        g = group_at(turn)

        @pl.when(i == 0)
        def _():
            wait_bytes(qin.at[0], local_sem.at[2])

        @pl.when(i < HEADS)
        def _():
            wait_bytes(qin.at[pl.ds(0, 3), :, pl.ds(0, HEAD_DIM)], q_recv.at[g, h])

        @pl.when(i >= HEADS)
        def _():
            wait_bytes(qin.at[pl.ds(0, 4), :, pl.ds(0, HEAD_DIM)], q_recv.at[g, h])

        rows = qin[pl.ds(4 * g, 4), :, pl.ds(pl.multiple_of(h * HEAD_DIM, 128), HEAD_DIM)].reshape(BQ, HEAD_DIM)
        scaled = jnp.transpose(rows).astype(jnp.float32) * SCALE
        high = scaled.astype(jnp.bfloat16)
        qt[i, pl.ds(0, 128), :] = high
        qt[i, pl.ds(128, 128), :] = (scaled - high.astype(jnp.float32)).astype(jnp.bfloat16)

    def place(t):
        late = t - closing
        once = 2 * EARLY_BLOCKS
        rest = QBLOCKS - EARLY_BLOCKS
        near = (c >= 1) & (((t >= EARLY_BLOCKS) & (t < once)) | (t >= once + rest))
        skipped = jnp.where((c >= 1) & (t >= EARLY_BLOCKS), jnp.where(t >= once + rest, QBLOCKS, EARLY_BLOCKS), 0)
        stream = jnp.where(late < 0, jnp.where(near, NEAR, OWN), jnp.where(late % ways == 0, CACHE, FAR))
        block = jnp.where(late < 0, t - skipped, QBLOCKS - 1 - late // ways)
        return stream, block

    def masked(stream, p, piece):
        return jnp.where((stream == CACHE) & (2 * piece + p >= limit), MASKED, 0.0).astype(jnp.float32)

    def score_part(stream, queries, into, ch, best):
        p, start = divmod(ch * SUB, HALF)
        keys = kv[stream, p, 0, pl.ds(start, SUB), :]
        part = jnp.dot(jnp.concatenate([keys, keys], axis=1), queries, preferred_element_type=jnp.float32)
        into[pl.ds(ch * SUB, SUB), :] = part
        for b in range(SUB // TOK):
            here = jnp.max(part[b * TOK:(b + 1) * TOK].reshape(TOK // 8, 8, BQ), axis=0)
            here = here - masked(stream, p, (start + b * TOK) // TOK)
            best = here if best is None else jnp.maximum(best, here)
        return best

    def raised(block, best):
        old = top[block, 0:1, :]
        return old, jnp.maximum(old, jnp.max(best, axis=0, keepdims=True))

    def arrivals(t):
        @pl.when((t < EARLY_BLOCKS) | ((c == 0) & (t < QBLOCKS)))
        def _():
            take_q(t)

        @pl.when((c >= 1) & (t >= 2 * EARLY_BLOCKS) & (t < EARLY_BLOCKS + QBLOCKS))
        def _():
            take_q(t - EARLY_BLOCKS)

        for at, turn, head in Q_SENT:
            @pl.when(t == at)
            def _(turn=turn, head=head):
                send_q(turn, head)

        @pl.when(t == CACHE_SENT)
        def _():
            send_kv(CACHE)

        @pl.when(t == jnp.where(c == 0, QBLOCKS - 1, CACHE_STEP))
        def _():
            take_kv(CACHE, True)
            take_kv(CACHE, False)

        for which, at in enumerate(NEAR_STEPS):
            @pl.when((t == at) & (c >= 1))
            def _(which=which):
                take_window(NEAR, which == 0)

        for which, at in enumerate(FAR_STEPS):
            @pl.when((t == at) & (c >= 2))
            def _(which=which):
                take_window(FAR, which == 0)

        @pl.when((t == EARLY_BLOCKS) & (c >= 1))
        def _():
            take_side(NEAR)

        @pl.when(t == closing)
        def _():
            take_side(CACHE)

        @pl.when((t == closing + 1) & (c >= 2))
        def _():
            take_side(FAR)

    def finish(block):
        summed = acc[block]
        whole = jnp.sum(total[block], axis=0, keepdims=True)
        square = jnp.mean(summed * summed, axis=0, keepdims=True)
        normed = summed * lax.rsqrt(square + 1e-06 * (whole * whole))
        turn, h = turn_of(block)
        g = group_at(turn)
        scale = jnp.concatenate([gates[h]] * (BQ // HEAD_DIM), axis=1)
        stage[block] = jnp.transpose((normed * scale).astype(jnp.bfloat16))
        wanted = out.at[0, :, pl.ds(pl.multiple_of((HEADS * slot + h) * HEAD_DIM, 128), HEAD_DIM)]
        for e in range(4):
            there = 4 * g + e
            held = stage.at[block, pl.ds(e * TOK, TOK)]

            @pl.when(there == s)
            def _():
                pltpu.make_async_copy(held, wanted, out_local).start()

            @pl.when(there != s)
            def _():
                pltpu.make_async_remote_copy(
                    src_ref=held, dst_ref=wanted, send_sem=out_send, recv_sem=out_recv,
                    device_id={"span": c, "seq": there}, device_id_type=MESH,
                ).start()

    def step(t, now, later, best, last=False):
        old, new = best
        stream, block = place(t)
        top[block, 0:1, :] = new

        if not last:
            arrivals(t + 1)
            next_stream, next_block = place(t + 1)
            queries = qt[next_block]
        factor = jnp.exp2(old - new)
        best = None
        update = None
        sums = None
        for ch in range(SPAN_TOKENS // SUB):
            if not last:
                best = score_part(next_stream, queries, later, ch, best)
            p, start = divmod(ch * SUB, HALF)
            rounded = []
            for b in range(SUB // TOK):
                shift = new + masked(stream, p, (start + b * TOK) // TOK)
                weights = jnp.exp2(now[pl.ds(ch * SUB + b * TOK, TOK), :] - shift)
                part = jnp.sum(weights.reshape(TOK // 8, 8, BQ), axis=0)
                sums = part if sums is None else sums + part
                rounded.append(weights.astype(jnp.bfloat16))
            product = jnp.dot(
                vt[stream, :, pl.ds(ch * SUB, SUB)], jnp.concatenate(rounded, axis=0), preferred_element_type=jnp.float32
            )
            update = product if update is None else update + product
        acc[block] = acc[block] * factor + update
        total[block] = total[block] * factor + sums

        @pl.when((t >= closing) & ((t - closing) % ways == ways - 1))
        def _():
            finish(block)

        return None if last else raised(next_block, best)

    @pl.when(flip == 0)
    def _():
        pltpu.make_async_copy(gate, gate_rows, local_sem.at[3]).wait()

    @pl.when(flip == 1)
    def _():
        gate_copy.wait()

    level_rows = lax.broadcasted_iota(jnp.int32, gate_rows.shape, 0)
    chosen = jnp.sum(jnp.where(level_rows == levels[0], gate_rows[...], 0.0), axis=0, keepdims=True)
    for h in range(HEADS):
        gates[h] = jnp.transpose(jnp.broadcast_to(chosen[:, h * HEAD_DIM:(h + 1) * HEAD_DIM], (HEAD_DIM, HEAD_DIM)))

    take_kv(OWN, True)
    send_q(0, 1)
    send_q(0, 2)
    take_kv(OWN, False)
    send_q(1, 0)
    send_q(2, 0)
    take_q(jnp.int32(0))
    take_side(OWN)
    best = None
    for ch in range(SPAN_TOKENS // SUB):
        best = score_part(OWN, qt[0], s0, ch, best)
    best = raised(0, best)

    def pair(i, best):
        best = step(2 * i, s0, s1, best)
        return step(2 * i + 1, s1, s0, best)

    best = lax.fori_loop(0, steps // 2 - 1, pair, best)
    best = step(steps - 2, s0, s1, best)
    step(steps - 1, s1, s0, best, last=True)

    columns = (SEQ - 1) * QW
    wait_bytes(out.at[0, :, pl.ds(0, QW)], out_local)
    wait_bytes(x.at[0, :, pl.ds(0, columns)], q_send)
    wait_bytes(x.at[0, :, pl.ds(0, 14 * HEAD_DIM)], kv_send.at[OWN])
    wait_bytes(x.at[0, :, pl.ds(0, 14 * HEAD_DIM)], kv_send.at[CACHE])
    for part in range(2):
        side_copy(OWN, part).wait_send()
        side_copy(CACHE, part).wait_send()

        @pl.when(c < SPANS - 1)
        def _():
            pass_copy(OWN, part).wait_send()

        @pl.when(c >= 1)
        def _():
            side_copy(NEAR, part).wait_send()

        @pl.when((c >= 1) & (c < SPANS - 1))
        def _():
            pass_copy(NEAR, part).wait_send()

        @pl.when(c >= 2)
        def _():
            side_copy(FAR, part).wait_send()

    wait_bytes(out.at[0, :, pl.ds(0, columns)], out_send)
    wait_bytes(out.at[0, :, pl.ds(0, columns)], out_recv)


def on_device(projected, cache_kv, levels, cache_blocks, gate_table):
    cache_rows = cache_kv.reshape(TOK, 2 * KV_WIDTH)
    dma = pltpu.SemaphoreType.DMA
    return pl.pallas_call(
        kernel,
        out_shape=jax.ShapeDtypeStruct((1, TOK, MODEL_WIDTH), jnp.bfloat16),
        in_specs=[
            pl.BlockSpec(memory_space=pl.ANY),
            pl.BlockSpec(memory_space=pl.ANY),
            pl.BlockSpec(memory_space=pltpu.SMEM),
            pl.BlockSpec(memory_space=pltpu.SMEM),
            pl.BlockSpec(memory_space=pl.ANY),
        ],
        out_specs=pl.BlockSpec(memory_space=pl.ANY),
        scratch_shapes=[
            pltpu.VMEM((4, 2, 2, HALF, HEAD_DIM), jnp.bfloat16),
            pltpu.VMEM((4, HEAD_DIM, SPAN_TOKENS), jnp.bfloat16),
            pltpu.VMEM((SEQ, TOK, QW), jnp.bfloat16),
            pltpu.VMEM((QBLOCKS, 2 * HEAD_DIM, BQ), jnp.bfloat16),
            pltpu.VMEM((QBLOCKS, HEAD_DIM, BQ), jnp.float32),
            pltpu.VMEM((QBLOCKS, 8, BQ), jnp.float32),
            pltpu.VMEM((QBLOCKS, 8, BQ), jnp.float32),
            pltpu.VMEM((SPAN_TOKENS, BQ), jnp.float32),
            pltpu.VMEM((SPAN_TOKENS, BQ), jnp.float32),
            pltpu.VMEM((QBLOCKS, BQ, HEAD_DIM), jnp.bfloat16),
            pltpu.VMEM((HEADS, HEAD_DIM, HEAD_DIM), jnp.float32),
            pltpu.VMEM((16, QW), jnp.float32),
            dma((2,)), dma((2, 2)), dma((4,)), dma((4, 2)), dma((4, 2)), dma((2, 2)), dma((2, 2)),
            dma, dma((4, 3)), dma, dma, dma, dma((2,)),
        ],
        compiler_params=pltpu.CompilerParams(
            collective_id=0, has_side_effects=True, vmem_limit_bytes=50 * 2**20
        ),
    )(projected, cache_rows, levels, cache_blocks, gate_table)


def solution(mesh):
    placed = (P("span", "seq", None), P("seq", None, None), P("span"), P("span"), P(None, "seq"))
    return jax.shard_map(
        on_device, mesh=mesh, in_specs=placed, out_specs=P("span", "seq", None), check_vma=False
    )
```
